256 devices in a mesh: ctx: 64 (over z, x, core), enc: 4 (over y).
Axes of the slice: x: 4, y: 4, z: 8, core: 2. Of those that a mesh axis runs over, the one named last changes fastest.
Arguments:
- queries: bfloat16 [8192, 4096], P('ctx', 'enc'), may hold values from -6 to 6
- d_out: bfloat16 [8192, 4096], P('ctx', 'enc'), may hold values from -24 to 24
- states: bfloat16 [24, 128, 896], P('enc'), may hold values from -6 to 6
- w_key: bfloat16 [896, 4096], P(None, 'enc'), may hold values from -0.1875 to 0.1875
- w_value: bfloat16 [896, 4096], P(None, 'enc'), may hold values from -0.1875 to 0.1875
- nbr_owner: int32 [128, 2], P('ctx'), may hold values from 0 to 3, all different within a row; in each aligned block of 2 rows (0 to 1, 2 to 3, ...) at most 2 rows name the same one
- nbr_row: int32 [128, 2], P('ctx'), may hold values from 0 to 5
Outputs:
- d_query: bfloat16 [8192, 4096], P('ctx', 'enc')
- d_states: bfloat16 [24, 128, 896], P('enc')
- d_wkey: bfloat16 [896, 4096], P(None, 'enc')
- d_wvalue: bfloat16 [896, 4096], P(None, 'enc')
The draws below stay inside these ranges and needn't reach their ends.
Inputs may be any that keep to these rules, and one draw needn't show every extreme that they name: `nbr_owner`: within the 2 spans of one index of ctx no owner is named more than 2 times, and in every draw some index of ctx names some owner exactly 2 times; the 2 neighbours of one span have different owners.
All inputs are finite; a program needn't handle non-finite values.
Results may differ from the reference program's by a relative error of at most 0.01.
Values may be sent and summed in bfloat16 or wider, within the bound.
No kernel may reach another device: no remote copies, remote signals or barrier semaphores. Data moves between devices by JAX's collectives and lax.ppermute only.
A program may use at most 128 MiB of HBM per device.

```python
import math
import jax
import jax.numpy as jnp
import numpy as np
from jax import lax

HEADS = 32
HEAD = 128
ENC_W = 896
SPAN = 64
NTOK = 128
NBR = 2
CH_DEV = 2
TOKENS = 8192
SPANS = 128
CAP = 2
NB_DEV = 6
N_ENC = 4


def plant(result, own_key, smallest, largest):
    place = [jax.random.randint(jax.random.fold_in(own_key, axis), (), 0, length) for axis, length in enumerate(result.shape)]
    widest = result.shape.index(max(result.shape))
    neighbour = place[:widest] + [(place[widest] + 1) % result.shape[widest]] + place[widest + 1:]
    return result.at[tuple(place)].set(smallest).at[tuple(neighbour)].set(largest)


def block_scale(key, dims, shards, least, largest):
    gain, own = 1.0, jax.random.fold_in(key, 6)
    for dim, parts in shards:
        draws = jnp.exp(jax.random.uniform(jax.random.fold_in(own, dim), (parts,), jnp.float32, least / len(shards), largest / len(shards)))
        gain = gain * jnp.repeat(draws, dims[dim] // parts).reshape([-1 if axis == dim else 1 for axis in range(len(dims))])
    return gain


def rank_bounds(number_of, lean):
    weights = [(1 << 20) // math.isqrt(standing ** lean) + 1 for standing in range(1, number_of + 1)]
    scale = 1 + sum(weights) // (1 << 30)
    return np.cumsum(np.array([max(1, weight // scale) for weight in weights]))


def ranked(stream_key, dims, number_of, slope):
    grid = rank_bounds(number_of, slope)
    ticket = jax.random.randint(jax.random.fold_in(stream_key, 1), dims, 0, int(grid[number_of - 1]))
    standing = jnp.searchsorted(jnp.asarray(grid, jnp.int32), ticket, side="right")
    return jax.random.permutation(jax.random.fold_in(stream_key, 2), number_of)[standing].astype(jnp.int32)


def assign_block(own_key, own, number, rows, amount, top, limit, lean):
    sequence = jax.random.permutation(own_key, amount)
    crowded, common = load_shares(amount, rows * top, limit, lean, True), load_shares(amount, rows * top, limit, lean, False)
    places = jnp.arange(amount)

    def named(sizes, turn):
        used = int((sizes > 0).sum())
        fixed = max(1, used // 4)
        shifted = fixed + (places - fixed + turn * (used - fixed)) % max(1, amount - fixed)
        return jnp.zeros((amount,), jnp.int32).at[sequence[jnp.where(places < fixed, places, shifted)]].set(jnp.asarray(sizes, jnp.int32))

    sizes = jnp.where(number % 4 == 0, named(crowded, number // 4), named(common, number - number // 4 - 1))
    mixed = jax.random.permutation(jax.random.fold_in(own, 3), amount)
    donor, taker = mixed[0:amount // 2 * 2:2], mixed[1:amount // 2 * 2:2]
    slack = jnp.minimum(sizes[donor] - 1, limit - sizes[taker]) // 2
    slack = jnp.where((donor == sequence[0]) | (taker == sequence[0]) | (sizes[taker] == 0), 0, jnp.maximum(slack, 0))
    shifted = jax.random.randint(jax.random.fold_in(own, 4), (amount // 2,), 0, 1 << 20) % (slack + 1)
    sizes = sizes.at[donor].add(-shifted).at[taker].add(shifted)
    labels = jnp.searchsorted(jnp.cumsum(sizes), jnp.arange(rows * top), side="right").astype(jnp.int32)
    listing = labels.reshape(top, rows).T
    listing = listing[jax.random.permutation(jax.random.fold_in(own, 1), rows)]
    turn = jax.random.randint(jax.random.fold_in(own, 2), (rows, 1), 0, top)
    return jnp.take_along_axis(listing, (jnp.arange(top)[None, :] + turn) % top, axis=1)


def load_shares(count, total, bound, lean, full):
    portions = [(1 << 20) // math.isqrt(standing ** lean) + 1 for standing in range(1, count + 1)]
    largest = bound if full else min(bound, max(-(-total // count), total * portions[0] // sum(portions)))
    least = 1 if total - largest >= count - 1 else 0
    holding, spare = [largest] + [least] * (count - 1), total - largest - least * (count - 1)
    while spare > 0:
        free = [i for i in range(1, count) if holding[i] < largest] or [i for i in range(1, count) if holding[i] < bound]
        whole, remaining = sum([portions[i] for i in free]), spare
        for i in free:
            addition = min(bound - holding[i], max(1, remaining * portions[i] // whole), spare)
            holding[i] = holding[i] + addition
            spare = spare - addition
    return np.array(holding)


def noise(own_key, dims, spread, bound, pieces=(), kind=jnp.bfloat16):
    result = spread * jax.random.normal(own_key, dims, jnp.float32)
    if pieces:
        result = result * block_scale(own_key, dims, pieces, -0.22, 0.18)
    return jnp.clip(result, -bound, bound).astype(kind)


def setup_inputs(seed: int = 0) -> dict:
    splits = jax.random.split(jax.random.key(seed), 8)
    queries = noise(splits[0], (TOKENS, HEADS * HEAD), 1.0, 6.0, ((0, 64), (1, 4)))
    d_out = noise(splits[1], (TOKENS, HEADS * HEAD), 4.0, 24.0, ((0, 64), (1, 4)))
    states = noise(splits[2], (NB_DEV * N_ENC, NTOK, ENC_W), 1.0, 6.0, ((0, 4),))
    w_key = noise(splits[3], (ENC_W, HEADS * HEAD), ENC_W ** -0.5, 0.1875, ((1, 4),))
    w_value = noise(splits[4], (ENC_W, HEADS * HEAD), ENC_W ** -0.5, 0.1875, ((1, 4),))
    nbr_owner_keys = jax.random.split(jax.random.fold_in(splits[5], 1), SPANS // CH_DEV)
    nbr_owner_turns = jax.random.permutation(jax.random.fold_in(splits[5], 3), SPANS // CH_DEV)
    nbr_owner = jax.vmap(lambda own, number: assign_block(jax.random.fold_in(splits[5], 2), own, number, CH_DEV, N_ENC, NBR, CAP, 2))(nbr_owner_keys, nbr_owner_turns).reshape((SPANS, NBR))
    nbr_row = plant(ranked(splits[6], (SPANS, NBR), NB_DEV, 2), jax.random.fold_in(splits[6], 3), 0, NB_DEV - 1).astype(jnp.int32)
    return dict(queries=queries, d_out=d_out, states=states, w_key=w_key, w_value=w_value, nbr_owner=nbr_owner, nbr_row=nbr_row)


def reference(queries, d_out, states, w_key, w_value, nbr_owner, nbr_row):
    scaling = 1.0 / math.sqrt(HEAD)
    head_width = HEADS * HEAD
    pool_rows = NB_DEV * N_ENC
    neighbour_rows = (nbr_owner * NB_DEV + nbr_row).astype(jnp.int32)
    flat_states = states.reshape(pool_rows * NTOK, ENC_W)
    keys_pool = jnp.dot(flat_states, w_key, preferred_element_type=jnp.float32).astype(jnp.bfloat16)
    keys_pool = lax.optimization_barrier(keys_pool).reshape(pool_rows, NTOK, head_width)
    values_pool = jnp.dot(flat_states, w_value, preferred_element_type=jnp.float32).astype(jnp.bfloat16)
    values_pool = lax.optimization_barrier(values_pool).reshape(pool_rows, NTOK, head_width)
    padding = jnp.zeros((SPAN - 1, head_width), queries.dtype)
    query_rows = jnp.concatenate([queries[SPAN - 1:], padding], 0).reshape(SPANS, SPAN, HEADS, HEAD)
    grad_rows = jnp.concatenate([d_out[SPAN - 1:], padding], 0).reshape(SPANS, SPAN, HEADS, HEAD)
    zeros_pool = jnp.zeros((pool_rows, NTOK, head_width), jnp.float32)

    def one_span(running, inputs):
        keys_sum, values_sum = running
        query_block, grad_block, chosen = inputs
        key_block = keys_pool[chosen].reshape(NBR * NTOK, HEADS, HEAD).astype(jnp.float32)
        value_block = values_pool[chosen].reshape(NBR * NTOK, HEADS, HEAD).astype(jnp.float32)
        query_wide = query_block.astype(jnp.float32)
        grad_wide = grad_block.astype(jnp.float32)
        scores = jnp.einsum('qhd,khd->hqk', query_wide, key_block) * scaling
        exponent_terms = jnp.exp(scores)
        soft_weights = exponent_terms / lax.optimization_barrier(jnp.sum(exponent_terms, axis=-1, keepdims=True))
        soft_rounded = lax.optimization_barrier(soft_weights.astype(jnp.bfloat16)).astype(jnp.float32)
        attended = jnp.einsum('hqk,khd->qhd', soft_rounded, value_block)
        delta_rows = lax.optimization_barrier(jnp.sum(grad_wide * attended, axis=-1))
        value_grad = jnp.einsum('hqk,qhd->khd', soft_rounded, grad_wide).astype(jnp.bfloat16)
        soft_grad = jnp.einsum('qhd,khd->hqk', grad_wide, value_block)
        score_grad = soft_weights * (soft_grad - jnp.transpose(delta_rows)[:, :, None])
        score_rounded = lax.optimization_barrier(score_grad.astype(jnp.bfloat16)).astype(jnp.float32)
        query_grad = (jnp.einsum('hqk,khd->qhd', score_rounded, key_block) * scaling).astype(jnp.bfloat16)
        key_grad = (jnp.einsum('hqk,qhd->khd', score_rounded, query_wide) * scaling).astype(jnp.bfloat16)
        key_grad = lax.optimization_barrier(key_grad).astype(jnp.float32)
        value_grad = lax.optimization_barrier(value_grad).astype(jnp.float32)
        keys_sum = keys_sum.at[chosen].add(key_grad.reshape(NBR, NTOK, head_width))
        values_sum = values_sum.at[chosen].add(value_grad.reshape(NBR, NTOK, head_width))
        return ((keys_sum, values_sum), query_grad.reshape(SPAN, head_width))
    sums, query_grads = lax.scan(one_span, (zeros_pool, zeros_pool), (query_rows, grad_rows, neighbour_rows))
    keys_sum, values_sum = sums
    flat_grads = query_grads.reshape(SPANS * SPAN, head_width)
    d_query = jnp.concatenate([padding, flat_grads[:TOKENS - (SPAN - 1)]], 0)
    wkey_wide = w_key.astype(jnp.float32)
    wvalue_wide = w_value.astype(jnp.float32)
    states_wide = states.astype(jnp.float32)
    d_states = jnp.einsum('rtd,fd->rtf', keys_sum, wkey_wide, precision=lax.Precision.HIGHEST)
    d_states = d_states + jnp.einsum('rtd,fd->rtf', values_sum, wvalue_wide, precision=lax.Precision.HIGHEST)
    d_wkey = jnp.einsum('rtf,rtd->fd', states_wide, keys_sum, precision=lax.Precision.HIGHEST)
    d_wvalue = jnp.einsum('rtf,rtd->fd', states_wide, values_sum, precision=lax.Precision.HIGHEST)
    return (d_query, d_states.astype(jnp.bfloat16), d_wkey.astype(jnp.bfloat16), d_wvalue.astype(jnp.bfloat16))
```

```python
import functools
import math

import jax
import jax.numpy as jnp
from jax import lax
from jax.experimental import pallas as pl
from jax.experimental.pallas import tpu as pltpu
from jax.sharding import PartitionSpec as P

HEAD = 128
SPAN = 64
NX, NZ, NY = 4, 8, 4
BF = jnp.bfloat16
F4 = jnp.float32
VMEM = pl.BlockSpec(memory_space=pltpu.VMEM)
SMEM = pl.BlockSpec(memory_space=pltpu.SMEM)
ANYS = pl.BlockSpec(memory_space=pl.ANY)
ORDER = (2, 1, 3, 0)
PARAMS = pltpu.CompilerParams(vmem_limit_bytes=56 * 1024 * 1024)


def move(a, place):
    pairs = []
    for i in range(NZ * NX * 2):
        z, x, c = place(i // 8, (i // 2) % NX, i % 2)
        pairs.append((i, (z % NZ) * 8 + (x % NX) * 2 + c))
    return lax.ppermute(a, "ctx", pairs)


def to_x(a, k):
    return move(a, lambda z, x, c: (z, x + k, c))


def to_z(a, k):
    return move(a, lambda z, x, c: (z + k, x, c))


def to_core(a):
    return move(a, lambda z, x, c: (z, x, 1 - c))


def to_y(a, k):
    return lax.ppermute(a, "enc", [(i, (i + k) % NY) for i in range(NY)])


def shape(dims, dtype=BF):
    return jax.ShapeDtypeStruct(dims, dtype)


def pick_kernel(place_ref, owner_ref, row_ref, states_ref, out0, out1, sems):
    me = place_ref[0]
    seen = jnp.int32(0)
    first = jnp.int32(0)
    second = jnp.int32(0)
    for u in range(4):
        hit = owner_ref[u] == me
        row = row_ref[u]
        first = jnp.where(hit & (seen == 0), row, first)
        second = jnp.where(hit & (seen == 1), row, second)
        seen = seen + hit.astype(jnp.int32)
    a = pltpu.make_async_copy(states_ref.at[first], out0, sems.at[0])
    b = pltpu.make_async_copy(states_ref.at[second], out1, sems.at[1])
    a.start()
    b.start()
    a.wait()
    b.wait()


def rows_kernel(slot_ref, *refs):
    slots, out = refs[:8], refs[8]
    for u in range(4):
        for s in range(8):

            @pl.when(slot_ref[u] == s)
            def _():
                out[u * 128 : (u + 1) * 128, :] = slots[s][...]


def dot(a, b, da, db):
    return lax.dot_general(a, b, (((da,), (db,)), ((), ())), preferred_element_type=F4)


def main_kernel(
    info_ref, rows_ref, wk_ref, wv_ref, q_ref, g_ref,
    keep_ref, send_ref, dq_ref, s0_ref, s1_ref, s2_ref, s3_ref, acc_ref,
):
    step = pl.program_id(0)
    scaling = 1.0 / math.sqrt(HEAD)
    core = info_ref[5]
    rows = rows_ref[...]
    wk = wk_ref[...]
    wv = wv_ref[...]
    keys = dot(rows, wk, 1, 0).astype(BF)
    values = dot(rows, wv, 1, 0).astype(BF)
    dk_spans = []
    dv_spans = []
    for s in range(2):
        dk_heads = []
        dv_heads = []
        for h in range(2):
            cols = slice(h * HEAD, (h + 1) * HEAD)
            q = q_ref[s * SPAN : (s + 1) * SPAN, cols]
            g = g_ref[s * SPAN : (s + 1) * SPAN, cols]
            k = keys[s * 256 : (s + 1) * 256, cols]
            v = values[s * 256 : (s + 1) * 256, cols]
            e = jnp.exp(dot(q, k, 1, 1) * scaling)
            soft = e / jnp.sum(e, axis=-1, keepdims=True)
            rounded = soft.astype(BF)
            soft_grad = dot(g, v, 1, 1)
            delta = jnp.sum(rounded.astype(F4) * soft_grad, axis=-1, keepdims=True)
            score_grad = (soft * (soft_grad - delta)).astype(BF)
            dq_ref[s * SPAN : (s + 1) * SPAN, cols] = (
                dot(score_grad, k, 1, 0) * scaling
            ).astype(BF)
            dk_heads.append((dot(score_grad, q, 0, 0) * scaling).astype(BF))
            dv_heads.append(dot(rounded, g, 0, 0).astype(BF))
        dk_spans.append(jnp.concatenate(dk_heads, axis=1))
        dv_spans.append(jnp.concatenate(dv_heads, axis=1))
    dk = jnp.concatenate(dk_spans, axis=0)
    dv = jnp.concatenate(dv_spans, axis=0)
    keep_ref[0] = jnp.where(core == 0, dk, dv)
    send_ref[0] = jnp.where(core == 0, dv, dk)
    part = dot(dk, wk, 1, 1) + dot(dv, wv, 1, 1)

    @pl.when(step == 0)
    def _():
        acc_ref[...] = part

    @pl.when(step > 0)
    def _():
        acc_ref[...] += part

    @pl.when(step == 3)
    def _():
        for o, out in enumerate((s0_ref, s1_ref, s2_ref, s3_ref)):
            for r in range(2):
                out[r] = jnp.zeros((128, 896), BF)
                for u in range(4):

                    @pl.when(info_ref[6 + u] == o * 2 + r)
                    def _():
                        out[r] = acc_ref[u * 128 : (u + 1) * 128, :].astype(BF)


def weight_kernel(rows_ref, other_ref, keep_ref, recv_ref, *outs):
    mine = rows_ref[...]
    other = other_ref[...]
    for k in range(4):
        total = dot(mine, keep_ref[k], 0, 0) + dot(other, recv_ref[k], 0, 0)
        total = total.astype(BF)
        outs[2 * k][...] = total[:448]
        outs[2 * k + 1][...] = total[448:]


def pack_kernel(info_ref, *refs):
    pt, ut, vt, pb, ub, vb, d0, d1, d2, d3 = refs[:10]
    outs = refs[10:18]
    full = refs[18]
    f = lambda r: r[...].astype(F4)
    full[:448, :256] = (f(pt) + f(ut) + f(vt)).astype(BF)
    full[448:, :256] = (f(pb) + f(ub) + f(vb)).astype(BF)
    for r in range(6):
        for g in range(7):
            cols = slice(g * 128, (g + 1) * 128)
            total = (
                d0[r, :, cols].astype(F4)
                + d1[r, :, cols].astype(F4)
                + d2[r, :, cols].astype(F4)
                + d3[r, :, cols].astype(F4)
            )
            start = r * 112 + g * 16
            full[start : start + 16, 256:] = total.astype(BF)
    full[672:, 256:] = jnp.zeros((224, 128), BF)
    z = info_ref[3]
    for k in range(NZ):
        at = lax.rem(z + k, NZ) * 112
        outs[k][...] = full[pl.ds(pl.multiple_of(at, 16), 112), :]


def final_kernel(info_ref, *refs):
    pieces = refs[:16]
    wkey, wvalue, dstates = refs[16:]
    x, z, core = info_ref[4], info_ref[3], info_ref[5]
    for p in range(2):
        owner = core if p == 0 else 1 - core
        for k in range(4):
            cols = pl.ds(pl.multiple_of(lax.rem(x + k, 4) * 256, 256), 256)
            tokens = pl.ds(pl.multiple_of(owner * 64 + lax.rem(x + k, 4) * 16, 16), 16)
            for m in range(8):
                piece = pieces[p * 8 + k * 2 + m // 4]
                at = slice((m % 4) * 112, (m % 4 + 1) * 112)
                where = lax.rem(z - m + NZ, NZ)
                rows = pl.ds(pl.multiple_of(where * 112, 16), 112)

                @pl.when(owner == 0)
                def _():
                    wkey[rows, cols] = piece[at, :256]

                @pl.when(owner == 1)
                def _():
                    wvalue[rows, cols] = piece[at, :256]

                @pl.when(where < 6)
                def _():
                    for g in range(7):
                        dstates[where, tokens, g * 128 : (g + 1) * 128] = piece[
                            at.start + g * 16 : at.start + (g + 1) * 16, 256:
                        ]


def local(queries, d_out, states, w_key, w_value, nbr_owner, nbr_row):
    me = lax.axis_index("enc").astype(jnp.int32)
    ctx = lax.axis_index("ctx").astype(jnp.int32)
    z, x, core = ctx // 8, (ctx // 2) % NX, ctx % 2
    token_count, head_width = queries.shape
    margin = SPAN - 1
    owners = nbr_owner.reshape(-1)
    rows_in = nbr_row.reshape(-1)

    own0, own1 = pl.pallas_call(
        pick_kernel,
        out_shape=(shape((128, 896)), shape((128, 896))),
        in_specs=[SMEM, SMEM, SMEM, ANYS],
        out_specs=(VMEM, VMEM),
        scratch_shapes=[pltpu.SemaphoreType.DMA((2,))],
        compiler_params=PARAMS,
    )(me.reshape(1), owners, rows_in, states)
    low0 = to_y(own0, 1)
    high1 = to_y(own1, -1)
    low1 = to_y(own1, 1)
    high0 = to_y(own0, -1)
    far0 = to_y(low0, 1)
    far1 = to_y(high1, -1)

    order = jnp.arange(4, dtype=jnp.int32)
    rank = jnp.sum(
        ((owners[:, None] == owners[None, :]) & (order[None, :] < order[:, None])).astype(jnp.int32),
        axis=1,
    )
    slots = jnp.remainder(owners - me, NY) * 2 + rank
    mine = (owners[None, :] == me) & (rank[None, :] == order[:2, None])
    owned = jnp.sum(jnp.where(mine, rows_in[None, :] + 1, 0), axis=1) - 1
    owned_other = to_core(owned)
    rel = [jnp.remainder(x + k, NX) for k in ORDER]
    info = jnp.concatenate([jnp.stack(rel[:3] + [z, x, core]), slots]).astype(jnp.int32)

    tail_q, tail_g = (
        lax.ppermute(a[:margin], "ctx", [(i, i - 1) for i in range(1, NZ * NX * 2)])
        for a in (queries, d_out)
    )
    q_rows = jnp.concatenate([queries[margin:], tail_q], 0)
    g_rows = jnp.concatenate([d_out[margin:], tail_g], 0)

    use_rows = pl.pallas_call(
        rows_kernel,
        out_shape=shape((512, 896)),
        in_specs=[SMEM] + [VMEM] * 8,
        out_specs=VMEM,
        compiler_params=PARAMS,
    )(slots, own0, own1, high0, high1, far0, far1, low0, low1)
    other_rows = to_core(use_rows)

    block = lambda j, info: (0, lax.rem(info[4] + jnp.where(j < 2, 2 - j, jnp.where(j == 2, 3, 0)), 4))
    whole = lambda j, info: (0, 0)
    slab = lambda j, info: (j, 0, 0)
    fixed3 = lambda j, info: (0, 0, 0)
    keep, send, dq, s0, s1, s2, s3 = pl.pallas_call(
        main_kernel,
        grid_spec=pltpu.PrefetchScalarGridSpec(
            num_scalar_prefetch=1,
            grid=(4,),
            in_specs=[
                pl.BlockSpec((512, 896), whole),
                pl.BlockSpec((896, 256), block),
                pl.BlockSpec((896, 256), block),
                pl.BlockSpec((128, 256), block),
                pl.BlockSpec((128, 256), block),
            ],
            out_specs=[
                pl.BlockSpec((1, 512, 256), slab),
                pl.BlockSpec((1, 512, 256), slab),
                pl.BlockSpec((128, 256), block),
            ]
            + [pl.BlockSpec((2, 128, 896), fixed3)] * 4,
            scratch_shapes=[pltpu.VMEM((512, 896), F4)],
        ),
        out_shape=[shape((4, 512, 256)), shape((4, 512, 256)), shape((128, 1024))]
        + [shape((2, 128, 896))] * 4,
        compiler_params=PARAMS,
    )(info, use_rows, w_key, w_value, q_rows, g_rows)

    got = to_core(send)
    e1 = to_y(s1, 1)
    e3 = to_y(s3, -1)
    e2 = to_y(s2, 2)

    p2t, p2b, p1t, p1b, p3t, p3b, p0t, p0b = pl.pallas_call(
        weight_kernel,
        out_shape=[shape((448, 256))] * 8,
        in_specs=[VMEM] * 4,
        out_specs=[VMEM] * 8,
        compiler_params=PARAMS,
    )(use_rows, other_rows, keep, got)
    add = lambda a, b: (a.astype(F4) + b.astype(F4)).astype(BF)
    ra = to_x(p2t, 1)
    rb = to_x(p2b, -1)
    ub = to_x(p1b, 1)
    vt = to_x(p3t, -1)
    ut = to_x(add(p1t, ra), 1)
    vb = to_x(add(p3b, rb), -1)

    earlier = lax.ppermute(
        dq[token_count - margin :], "ctx", [(i, i + 1) for i in range(NZ * NX * 2 - 1)]
    )
    d_query = jnp.concatenate([earlier, dq[: token_count - margin]], 0)

    wide = lambda a: a.astype(F4)
    slot_sum = wide(s0) + wide(e1) + wide(e2) + wide(e3)
    half = lambda c: lax.dynamic_slice_in_dim(slot_sum, c * 64, 64, axis=1)
    theirs = half(1 - core).astype(BF)
    ours = half(core)
    theirs = to_core(theirs)
    pool = jnp.arange(6, dtype=jnp.int32)[:, None, None]
    zero = jnp.zeros((), F4)
    pool_sum = sum(
        jnp.where(pool == owned[s], ours[s][None], zero)
        + jnp.where(pool == owned_other[s], wide(theirs[s])[None], zero)
        for s in range(2)
    ).astype(BF)
    piece = lambda k: lax.dynamic_slice_in_dim(pool_sum, ((x + k) % NX) * 16, 16, axis=1)
    d1 = to_x(piece(1), 1)
    d3 = to_x(piece(3), -1)
    d2 = to_x(piece(2), 2)
    d0 = piece(0)

    chunks = pl.pallas_call(
        pack_kernel,
        out_shape=[shape((112, 384))] * 8,
        in_specs=[SMEM] + [VMEM] * 10,
        out_specs=[VMEM] * 8,
        scratch_shapes=[pltpu.VMEM((896, 384), BF)],
        compiler_params=PARAMS,
    )(info, p0t, ut, vt, p0b, ub, vb, d0, d1, d2, d3)
    total = wide(chunks[0])
    for k in (1, 7, 2, 6, 3, 5, 4):
        total = total + wide(to_z(chunks[k], k))
    total = total.astype(BF)

    ring = {0: total}
    for k in (1, 7, 2, 6, 3, 5, 4):
        ring[k] = to_z(total, k)
    top = jnp.concatenate([ring[k] for k in range(4)], 0)
    bot = jnp.concatenate([ring[k] for k in range(4, 8)], 0)

    lt = to_x(top, 1)
    hb = to_x(bot, -1)
    lb = to_x(bot, 1)
    ht = to_x(top, -1)
    ft = to_x(lt, 1)
    fb = to_x(hb, -1)
    ours = [top, bot, ht, hb, ft, fb, lt, lb]
    theirs = [to_core(a) for a in ours]
    d_wkey, d_wvalue, d_states = pl.pallas_call(
        final_kernel,
        out_shape=[shape((896, 1024)), shape((896, 1024)), shape((6, 128, 896))],
        in_specs=[SMEM] + [VMEM] * 16,
        out_specs=[VMEM] * 3,
        compiler_params=PARAMS,
    )(info, *ours, *theirs)
    return d_query, d_states, d_wkey, d_wvalue


def solution(mesh):
    return jax.shard_map(
        local,
        mesh=mesh,
        in_specs=(
            P("ctx", "enc"),
            P("ctx", "enc"),
            P("enc", None, None),
            P(None, "enc"),
            P(None, "enc"),
            P("ctx", None),
            P("ctx", None),
        ),
        out_specs=(P("ctx", "enc"), P("enc", None, None), P(None, "enc"), P(None, "enc")),
        check_vma=False,
    )
```

```python
import functools
import math

import jax
import jax.numpy as jnp
from jax import lax
from jax.experimental import pallas as pl
from jax.experimental.pallas import tpu as pltpu
from jax.sharding import PartitionSpec as P

HEAD = 128
SPAN = 64
NX, NZ, NY = 4, 8, 4
BF = jnp.bfloat16
F4 = jnp.float32
VMEM = pl.BlockSpec(memory_space=pltpu.VMEM)
SMEM = pl.BlockSpec(memory_space=pltpu.SMEM)
ANYS = pl.BlockSpec(memory_space=pl.ANY)
ORDER = (2, 1, 3, 0)


def move(a, place):
    pairs = []
    for i in range(NZ * NX * 2):
        z, x, c = place(i // 8, (i // 2) % NX, i % 2)
        pairs.append((i, (z % NZ) * 8 + (x % NX) * 2 + c))
    return lax.ppermute(a, "ctx", pairs)


def to_x(a, k):
    return move(a, lambda z, x, c: (z, x + k, c))


def to_z(a, k):
    return move(a, lambda z, x, c: (z + k, x, c))


def to_core(a):
    return move(a, lambda z, x, c: (z, x, 1 - c))


def to_y(a, k):
    return lax.ppermute(a, "enc", [(i, (i + k) % NY) for i in range(NY)])


def shape(dims, dtype=BF):
    return jax.ShapeDtypeStruct(dims, dtype)


def after(a, *others):
    return lax.optimization_barrier((a, *others))[0]


def limit(mib):
    return pltpu.CompilerParams(vmem_limit_bytes=mib * 1024 * 1024)


def far(a):
    return pltpu.with_memory_space_constraint(a, pltpu.HBM)


def near(dims, dtype=BF):
    return pltpu.VMEM(dims, dtype)


def call(kernel, outs, scalars, arrays, scratch=(), mib=8):
    arrays = [pltpu.with_memory_space_constraint(a, pltpu.VMEM) for a in arrays]
    return pl.pallas_call(
        kernel,
        out_shape=outs,
        in_specs=[SMEM] * len(scalars) + [VMEM] * len(arrays),
        out_specs=[VMEM] * len(outs),
        scratch_shapes=list(scratch),
        compiler_params=limit(mib),
    )(*scalars, *arrays)


def dot(a, b, da, db):
    return lax.dot_general(a, b, (((da,), (db,)), ((), ())), preferred_element_type=F4)


def pick_kernel(owner_ref, row_ref, states_ref, out0, out1, owners, rows, sems):
    a = pltpu.make_async_copy(owner_ref, owners, sems.at[0])
    b = pltpu.make_async_copy(row_ref, rows, sems.at[1])
    a.start()
    b.start()
    a.wait()
    b.wait()
    me = lax.axis_index("enc")
    seen = jnp.int32(0)
    first = jnp.int32(0)
    second = jnp.int32(0)
    for u in range(4):
        hit = owners[u // 2, u % 2] == me
        row = rows[u // 2, u % 2]
        first = jnp.where(hit & (seen == 0), row, first)
        second = jnp.where(hit & (seen == 1), row, second)
        seen = seen + hit.astype(jnp.int32)
    a = pltpu.make_async_copy(states_ref.at[first], out0, sems.at[2])
    b = pltpu.make_async_copy(states_ref.at[second], out1, sems.at[3])
    a.start()
    b.start()
    a.wait()
    b.wait()


def fetch_kernel(*refs):
    sources, outs, sems = refs[:2], refs[2:4], refs[4]
    copies = [pltpu.make_async_copy(a, b, sems.at[n]) for n, (a, b) in enumerate(zip(sources, outs))]
    for copy in copies:
        copy.start()
    for copy in copies:
        copy.wait()


def rows_kernel(info_ref, *refs):
    slots, rows_ref, turned_ref = refs[:8], refs[8], refs[9]
    for u in range(4):
        for s in range(8):

            @pl.when(info_ref[5 + u] == s)
            def _():
                rows_ref[u * 128 : (u + 1) * 128, :] = slots[s][...]

    turned_ref[...] = rows_ref[...].T


def main_kernel(info_ref, *refs):
    rows_in, wk_ref, wv_ref, q_ref, g_ref = refs[:5]
    keep_ref, send_ref, dq_ref = refs[5:8]
    slot_outs = refs[8:12]
    dk_ref, dv_ref, acc_ref = refs[12:]
    scaling = 1.0 / math.sqrt(HEAD)
    core = info_ref[4]
    rows = rows_in[...]
    for pair in range(2):
        combos = []
        for j in (2 * pair, 2 * pair + 1):
            cols = pl.ds(pl.multiple_of(info_ref[j] * 256, 256), 256)
            keys = dot(rows, wk_ref[:, cols], 1, 0).astype(BF)
            values = dot(rows, wv_ref[:, cols], 1, 0).astype(BF)
            q_all = q_ref[:, cols]
            g_all = g_ref[:, cols]
            for s in range(2):
                for h in range(2):
                    here = slice(h * HEAD, (h + 1) * HEAD)
                    span = slice(s * SPAN, (s + 1) * SPAN)
                    uses = slice(s * 256, (s + 1) * 256)
                    combos.append(
                        (q_all[span, here], g_all[span, here], keys[uses, here], values[uses, here])
                    )
        scores = [dot(q, k, 1, 1) for q, g, k, v in combos]
        soft_grads = [dot(g, v, 1, 1) for q, g, k, v in combos]
        terms = [jnp.exp(a * scaling) for a in scores]
        softs = [e / jnp.sum(e, axis=-1, keepdims=True) for e in terms]
        rounded = [a.astype(BF) for a in softs]
        deltas = [
            jnp.sum(r.astype(F4) * d, axis=-1, keepdims=True) for r, d in zip(rounded, soft_grads)
        ]
        grads = [(p * (d - t)).astype(BF) for p, d, t in zip(softs, soft_grads, deltas)]
        dvs = [dot(r, c[1], 0, 0).astype(BF) for r, c in zip(rounded, combos)]
        dqs = [(dot(d, c[2], 1, 0) * scaling).astype(BF) for d, c in zip(grads, combos)]
        dks = [(dot(d, c[0], 0, 0) * scaling).astype(BF) for d, c in zip(grads, combos)]
        for m in range(2):
            j = 2 * pair + m
            cols = pl.ds(pl.multiple_of(info_ref[j] * 256, 256), 256)

            def join(parts):
                one, two = parts[4 * m : 4 * m + 2], parts[4 * m + 2 : 4 * m + 4]
                return jnp.concatenate(
                    [jnp.concatenate(one, axis=1), jnp.concatenate(two, axis=1)], axis=0
                )

            dq_ref[:, cols] = join(dqs)
            dk = join(dks)
            dv = join(dvs)
            dk_ref[:, cols] = dk
            dv_ref[:, cols] = dv
            keep_ref[j] = jnp.where(core == 0, dk, dv)
            send_ref[j] = jnp.where(core == 0, dv, dk)
    acc_ref[...] = dot(dk_ref[...], wk_ref[...], 1, 1) + dot(dv_ref[...], wv_ref[...], 1, 1)
    for o, out in enumerate(slot_outs):
        for r in range(2):
            out[r] = jnp.zeros((128, 896), BF)
            for u in range(4):

                @pl.when(info_ref[5 + u] == o * 2 + r)
                def _():
                    out[r] = acc_ref[u * 128 : (u + 1) * 128, :].astype(BF)


def weight_kernel(which, turned_ref, other_ref, keep_ref, got_ref, *outs):
    turned = turned_ref[...]
    other = other_ref[...]
    for n, k in enumerate(which):
        total = dot(turned, keep_ref[k], 1, 0) + dot(other, got_ref[k], 1, 0)
        outs[n][...] = total.astype(BF)


def slot_kernel(info_ref, s0, s1, s2, s3, ours, theirs):
    core = info_ref[2]
    for out, side in ((ours, core), (theirs, 1 - core)):
        tokens = pl.ds(pl.multiple_of(side * 64, 64), 64)
        f = lambda r, n: r[n, tokens, :].astype(F4)
        sums = [f(s0, n) + f(s1, n) + f(s2, n) + f(s3, n) for n in range(2)]
        for row in range(6):
            one = jnp.where(info_ref[3] == row, sums[0], 0.0)
            two = jnp.where(info_ref[4] == row, sums[1], 0.0)
            out[row] = (one + two).astype(BF)


def piece_kernel(info_ref, ours, theirs, *outs):
    x = info_ref[1]
    for k in range(NX):
        tokens = pl.ds(pl.multiple_of(lax.rem(x + k, NX) * 16, 16), 16)
        for row in range(6):
            total = ours[row, tokens, :].astype(F4) + theirs[row, tokens, :].astype(F4)
            outs[k][row] = total.astype(BF)


def join_kernel(p0, p1, p2, p3, d0, d1, d2, d3, out):
    f = lambda r: r[...].astype(F4)
    out[:, :256] = (f(p0) + f(p1) + f(p2) + f(p3)).astype(BF)
    for r in range(6):
        for g in range(7):
            cols = slice(g * 128, (g + 1) * 128)
            total = (
                d0[r, :, cols].astype(F4)
                + d1[r, :, cols].astype(F4)
                + d2[r, :, cols].astype(F4)
                + d3[r, :, cols].astype(F4)
            )
            start = r * 112 + g * 16
            out[start : start + 16, 256:] = total.astype(BF)
    out[672:, 256:] = jnp.zeros((224, 128), BF)


def total_kernel(got_ref, out):
    total = got_ref[0:112].astype(F4)
    for k in range(1, NZ):
        total = total + got_ref[k * 112 : (k + 1) * 112].astype(F4)
    out[...] = total.astype(BF)


def final_kernel(info_ref, *refs):
    ours, theirs = refs[:7], refs[7:14]
    wkey, wvalue, dstates = refs[14:17]
    full, pool, sems = refs[17:]
    z, x, core = info_ref[0], info_ref[1], info_ref[2]
    copies = []
    for p, pieces in enumerate((ours, theirs)):
        owner = core if p == 0 else 1 - core
        for k in range(4):
            cols = pl.ds(pl.multiple_of(lax.rem(x + k, 4) * 256, 256), 256)
            tokens = pl.ds(pl.multiple_of(owner * 64 + lax.rem(x + k, 4) * 16, 16), 16)
            for m in range(8):
                if k == 0:
                    piece, base = pieces[0], m * 112
                else:
                    piece, base = pieces[2 * k - 1 + m // 4], (m % 4) * 112
                where = lax.rem(z - m + NZ, NZ)
                rows = pl.ds(pl.multiple_of(where * 112, 16), 112)
                full[p, rows, cols] = piece[base : base + 112, :256]
                for g in range(7):
                    part = slice(g * 128, (g + 1) * 128)
                    pool[where, tokens, part] = piece[base + g * 16 : base + (g + 1) * 16, 256:]
        first = pltpu.make_async_copy(full.at[p], wkey, sems.at[p])
        second = pltpu.make_async_copy(full.at[p], wvalue, sems.at[p])

        @pl.when(owner == 0)
        def _():
            first.start()

        @pl.when(owner == 1)
        def _():
            second.start()

        copies.append((owner, first, second))
    last = pltpu.make_async_copy(pool.at[:6], dstates, sems.at[2])
    last.start()
    last.wait()
    for owner, first, second in copies:

        @pl.when(owner == 0)
        def _():
            first.wait()

        @pl.when(owner == 1)
        def _():
            second.wait()


def local(queries, d_out, states, w_key, w_value, nbr_owner, nbr_row):
    me = lax.axis_index("enc").astype(jnp.int32)
    ctx = lax.axis_index("ctx").astype(jnp.int32)
    z, x, core = ctx // 8, (ctx // 2) % NX, ctx % 2
    token_count, head_width = queries.shape
    margin = SPAN - 1
    z_groups = [[zz * 8 + rest for zz in range(NZ)] for rest in range(8)]
    swap_z = lambda a: lax.all_to_all(
        a, "ctx", split_axis=0, concat_axis=0, tiled=True, axis_index_groups=z_groups
    )

    own0, own1 = pl.pallas_call(
        pick_kernel,
        out_shape=(near((128, 896)), near((128, 896))),
        in_specs=[ANYS] * 3,
        out_specs=(VMEM, VMEM),
        scratch_shapes=[pltpu.SMEM((2, 2), jnp.int32), pltpu.SMEM((2, 2), jnp.int32)]
        + [pltpu.SemaphoreType.DMA((4,))],
        compiler_params=limit(8),
    )(far(nbr_owner), far(nbr_row), far(states))
    low0 = to_y(own0, 1)
    high1 = to_y(own1, -1)
    low1 = to_y(own1, 1)
    high0 = to_y(own0, -1)
    far0 = to_y(low0, 1)
    far1 = to_y(high1, -1)

    owners = nbr_owner.reshape(-1)
    rows_in = nbr_row.reshape(-1)
    order = jnp.arange(4, dtype=jnp.int32)
    rank = jnp.sum(
        ((owners[:, None] == owners[None, :]) & (order[None, :] < order[:, None])).astype(jnp.int32),
        axis=1,
    )
    slots = jnp.remainder(owners - me, NY) * 2 + rank
    mine = (owners[None, :] == me) & (rank[None, :] == order[:2, None])
    owned = jnp.sum(jnp.where(mine, rows_in[None, :] + 1, 0), axis=1) - 1
    rel = [jnp.remainder(x + k, NX) for k in ORDER]
    info = jnp.concatenate([jnp.stack(rel + [core]), slots]).astype(jnp.int32)
    places = jnp.concatenate([jnp.stack([z, x, core]), owned]).astype(jnp.int32)

    late_q, late_g = after(queries, low1), after(d_out, low1)
    tail_q, tail_g = (
        lax.ppermute(a[:margin], "ctx", [(i, i - 1) for i in range(1, NZ * NX * 2)])
        for a in (late_q, late_g)
    )
    q_rows = jnp.concatenate([late_q[margin:], tail_q], 0)
    g_rows = jnp.concatenate([late_g[margin:], tail_g], 0)
    fetched = pl.pallas_call(
        fetch_kernel,
        out_shape=[near((896, 1024)), near((896, 1024))],
        in_specs=[ANYS] * 2,
        out_specs=[VMEM] * 2,
        scratch_shapes=[pltpu.SemaphoreType.DMA((2,))],
        compiler_params=limit(8),
    )(far(after(w_key, low0)), far(after(w_value, low0)))

    rows, turned = call(
        rows_kernel,
        [near((512, 896)), near((896, 512))],
        [info],
        [own0, own1, high0, high1, far0, far1, low0, low1],
    )
    turned_other = to_core(turned)
    keep, send, dq, s0, s1, s2, s3 = call(
        main_kernel,
        [near((4, 512, 256)), near((4, 512, 256)), shape((128, 1024))] + [shape((2, 128, 896))] * 4,
        [info],
        [rows, *fetched, q_rows, g_rows],
        [pltpu.VMEM((512, 1024), BF), pltpu.VMEM((512, 1024), BF), pltpu.VMEM((512, 896), F4)],
        20,
    )
    got = to_core(send)
    e1 = to_y(s1, 1)
    e3 = to_y(s3, -1)
    e2 = to_y(s2, 2)

    def weights(which, keep):
        return call(
            functools.partial(weight_kernel, which),
            [near((896, 256))] * len(which),
            [],
            [turned, turned_other, keep, got],
        )

    p2, p1, p3 = weights((0, 1, 2), keep)
    (p0,) = weights((3,), after(keep, p2))
    p2, p1, p3 = to_x(p2, 2), to_x(p1, 1), to_x(p3, -1)

    e1, e2, e3, p0, p1, p2, p3 = lax.optimization_barrier((e1, e2, e3, p0, p1, p2, p3))
    ours, theirs = pl.pallas_call(
        slot_kernel,
        out_shape=[near((6, 64, 896))] * 2,
        in_specs=[SMEM] + [VMEM] * 4,
        out_specs=[VMEM] * 2,
        compiler_params=limit(8),
    )(places, s0, e1, e2, e3)
    theirs = to_core(theirs)
    d0, d1, d2, d3 = call(piece_kernel, [near((6, 16, 896))] * 4, [places], [ours, theirs])
    d1 = to_x(d1, 1)
    d3 = to_x(d3, -1)
    d2 = to_x(d2, 2)
    dq = after(dq, theirs)
    earlier = lax.ppermute(
        dq[token_count - margin :], "ctx", [(i, i + 1) for i in range(NZ * NX * 2 - 1)]
    )
    d_query = jnp.concatenate([earlier, dq[: token_count - margin]], 0)
    (joined,) = call(join_kernel, [near((896, 384))], [], [p0, p1, p2, p3, d0, d1, d2, d3])
    (total,) = call(total_kernel, [near((112, 384))], [], [swap_z(joined)])

    lo1 = to_z(total, 1)
    hi1 = to_z(total, -1)
    lo2 = to_z(total, 2)
    hi2 = to_z(total, -2)
    lo3 = to_z(lo1, 2)
    hi3 = to_z(hi1, -2)
    lo4 = to_z(lo2[:64], 2)
    hi4 = to_z(hi2[64:], -2)
    own = jnp.concatenate([total, lo1, lo2, lo3, lo4, hi4, hi3, hi2, hi1], 0)
    half = 448
    low_t = to_x(own[:half], 1)
    high_b = to_x(own[half:], -1)
    low_b = to_x(own[half:], 1)
    high_t = to_x(own[:half], -1)
    far_t = to_x(low_t, 1)
    far_b = to_x(high_b, -1)
    ours = [own, high_t, high_b, far_t, far_b, low_t, low_b]
    high_t, high_b, low_t, low_b, d_query, *_ = lax.optimization_barrier(
        (high_t, high_b, low_t, low_b, d_query, far_t, far_b)
    )
    theirs = [to_core(a) for a in (own, high_t, high_b, far_t, far_b, low_t, low_b)]
    arrays = ours + theirs
    d_wkey, d_wvalue, d_states = pl.pallas_call(
        final_kernel,
        out_shape=[shape((896, 1024)), shape((896, 1024)), shape((6, 128, 896))],
        in_specs=[SMEM] + [VMEM] * 14,
        out_specs=[ANYS] * 3,
        scratch_shapes=[pltpu.VMEM((2, 896, 1024), BF), pltpu.VMEM((8, 128, 896), BF)]
        + [pltpu.SemaphoreType.DMA((3,))],
        compiler_params=limit(8),
    )(places, *[pltpu.with_memory_space_constraint(a, pltpu.VMEM) for a in arrays])
    return d_query, d_states, d_wkey, d_wvalue


def solution(mesh):
    return jax.shard_map(
        local,
        mesh=mesh,
        in_specs=(
            P("ctx", "enc"),
            P("ctx", "enc"),
            P("enc", None, None),
            P(None, "enc"),
            P(None, "enc"),
            P("ctx", None),
            P("ctx", None),
        ),
        out_specs=(P("ctx", "enc"), P("enc", None, None), P(None, "enc"), P(None, "enc")),
        check_vma=False,
    )
```

```python
import functools
import math

import jax
import jax.numpy as jnp
from jax import lax
from jax.experimental import pallas as pl
from jax.experimental.pallas import tpu as pltpu
from jax.sharding import PartitionSpec as P

HEAD = 128
SPAN = 64
NX, NZ, NY = 4, 8, 4
BF = jnp.bfloat16
F4 = jnp.float32
VMEM = pl.BlockSpec(memory_space=pltpu.VMEM)
SMEM = pl.BlockSpec(memory_space=pltpu.SMEM)
ANYS = pl.BlockSpec(memory_space=pl.ANY)
ORDER = (2, 1, 3, 0)


def move(a, place):
    pairs = []
    for i in range(NZ * NX * 2):
        z, x, c = place(i // 8, (i // 2) % NX, i % 2)
        pairs.append((i, (z % NZ) * 8 + (x % NX) * 2 + c))
    return lax.ppermute(a, "ctx", pairs)


def to_x(a, k):
    return move(a, lambda z, x, c: (z, x + k, c))


def to_z(a, k):
    return move(a, lambda z, x, c: (z + k, x, c))


def to_core(a):
    return move(a, lambda z, x, c: (z, x, 1 - c))


def to_y(a, k):
    return lax.ppermute(a, "enc", [(i, (i + k) % NY) for i in range(NY)])


def shape(dims, dtype=BF):
    return jax.ShapeDtypeStruct(dims, dtype)


def after(a, *others):
    return lax.optimization_barrier((a, *others))[0]


def limit(mib):
    return pltpu.CompilerParams(vmem_limit_bytes=mib * 1024 * 1024)


def far(a):
    return pltpu.with_memory_space_constraint(a, pltpu.HBM)


def near(dims, dtype=BF):
    return pltpu.VMEM(dims, dtype)


def call(kernel, outs, scalars, arrays, scratch=(), mib=8):
    arrays = [pltpu.with_memory_space_constraint(a, pltpu.VMEM) for a in arrays]
    return pl.pallas_call(
        kernel,
        out_shape=outs,
        in_specs=[SMEM] * len(scalars) + [VMEM] * len(arrays),
        out_specs=[VMEM] * len(outs),
        scratch_shapes=list(scratch),
        compiler_params=limit(mib),
    )(*scalars, *arrays)


def dot(a, b, da, db):
    return lax.dot_general(a, b, (((da,), (db,)), ((), ())), preferred_element_type=F4)


def pick_kernel(owner_ref, row_ref, states_ref, out, owners, rows, sems):
    a = pltpu.make_async_copy(owner_ref, owners, sems.at[0])
    b = pltpu.make_async_copy(row_ref, rows, sems.at[1])
    a.start()
    b.start()
    a.wait()
    b.wait()
    me = lax.axis_index("enc")
    seen = jnp.int32(0)
    first = jnp.int32(0)
    second = jnp.int32(0)
    for u in range(4):
        hit = owners[u // 2, u % 2] == me
        row = rows[u // 2, u % 2]
        first = jnp.where(hit & (seen == 0), row, first)
        second = jnp.where(hit & (seen == 1), row, second)
        seen = seen + hit.astype(jnp.int32)
    a = pltpu.make_async_copy(states_ref.at[first], out.at[0], sems.at[2])
    b = pltpu.make_async_copy(states_ref.at[second], out.at[1], sems.at[3])
    a.start()
    b.start()
    a.wait()
    b.wait()


def fetch_kernel(*refs):
    sources, outs, sems = refs[:2], refs[2:4], refs[4]
    copies = [pltpu.make_async_copy(a, b, sems.at[n]) for n, (a, b) in enumerate(zip(sources, outs))]
    for copy in copies:
        copy.start()
    for copy in copies:
        copy.wait()


def rows_kernel(info_ref, *refs):
    slots, rows_ref, turned_ref = refs[:4], refs[4], refs[5]
    for u in range(4):
        for s in range(8):

            @pl.when(info_ref[5 + u] == s)
            def _():
                rows_ref[u * 128 : (u + 1) * 128, :] = slots[s // 2][s % 2]

    turned_ref[...] = rows_ref[...].T


def main_kernel(info_ref, *refs):
    rows_in, wk_ref, wv_ref, q_ref, g_ref = refs[:5]
    keep_ref, send_ref, dq_ref = refs[5:8]
    slot_outs = refs[8:12]
    dk_ref, dv_ref, acc_ref = refs[12:]
    scaling = 1.0 / math.sqrt(HEAD)
    core = info_ref[4]
    rows = rows_in[...]
    @pl.loop(0, 2)
    def _(pair):
        combos = []
        for m in range(2):
            j = 2 * pair + m
            cols = pl.ds(pl.multiple_of(info_ref[j] * 256, 256), 256)
            keys = dot(rows, wk_ref[:, cols], 1, 0).astype(BF)
            values = dot(rows, wv_ref[:, cols], 1, 0).astype(BF)
            q_all = q_ref[:, cols]
            g_all = g_ref[:, cols]
            for s in range(2):
                for h in range(2):
                    here = slice(h * HEAD, (h + 1) * HEAD)
                    span = slice(s * SPAN, (s + 1) * SPAN)
                    uses = slice(s * 256, (s + 1) * 256)
                    combos.append(
                        (q_all[span, here], g_all[span, here], keys[uses, here], values[uses, here])
                    )
        scores = [dot(q, k, 1, 1) for q, g, k, v in combos]
        soft_grads = [dot(g, v, 1, 1) for q, g, k, v in combos]
        terms = [jnp.exp(a * scaling) for a in scores]
        softs = [e / jnp.sum(e, axis=-1, keepdims=True) for e in terms]
        rounded = [a.astype(BF) for a in softs]
        deltas = [
            jnp.sum(r.astype(F4) * d, axis=-1, keepdims=True) for r, d in zip(rounded, soft_grads)
        ]
        grads = [(p * (d - t)).astype(BF) for p, d, t in zip(softs, soft_grads, deltas)]
        dvs = [dot(r, c[1], 0, 0).astype(BF) for r, c in zip(rounded, combos)]
        dqs = [(dot(d, c[2], 1, 0) * scaling).astype(BF) for d, c in zip(grads, combos)]
        dks = [(dot(d, c[0], 0, 0) * scaling).astype(BF) for d, c in zip(grads, combos)]
        for m in range(2):
            j = 2 * pair + m
            cols = pl.ds(pl.multiple_of(info_ref[j] * 256, 256), 256)

            def join(parts):
                one, two = parts[4 * m : 4 * m + 2], parts[4 * m + 2 : 4 * m + 4]
                return jnp.concatenate(
                    [jnp.concatenate(one, axis=1), jnp.concatenate(two, axis=1)], axis=0
                )

            dq_ref[:, cols] = join(dqs)
            dk = join(dks)
            dv = join(dvs)
            dk_ref[:, cols] = dk
            dv_ref[:, cols] = dv
            keep_ref[j] = jnp.where(core == 0, dk, dv)
            send_ref[j] = jnp.where(core == 0, dv, dk)

    acc_ref[...] = dot(dk_ref[...], wk_ref[...], 1, 1) + dot(dv_ref[...], wv_ref[...], 1, 1)
    for o, out in enumerate(slot_outs):
        for r in range(2):
            out[r] = jnp.zeros((128, 896), BF)
            for u in range(4):

                @pl.when(info_ref[5 + u] == o * 2 + r)
                def _():
                    out[r] = acc_ref[u * 128 : (u + 1) * 128, :].astype(BF)


def weight_kernel(which, turned_ref, other_ref, keep_ref, got_ref, *outs):
    turned = turned_ref[...]
    other = other_ref[...]
    for n, k in enumerate(which):
        total = dot(turned, keep_ref[k], 1, 0) + dot(other, got_ref[k], 1, 0)
        outs[n][...] = total.astype(BF)


def slot_kernel(info_ref, s0, s1, s2, s3, ours, theirs):
    core = info_ref[2]
    for out, side in ((ours, core), (theirs, 1 - core)):
        tokens = pl.ds(pl.multiple_of(side * 64, 64), 64)
        f = lambda r, n: r[n, tokens, :].astype(F4)
        sums = [f(s0, n) + f(s1, n) + f(s2, n) + f(s3, n) for n in range(2)]
        for row in range(6):
            one = jnp.where(info_ref[3] == row, sums[0], 0.0)
            two = jnp.where(info_ref[4] == row, sums[1], 0.0)
            out[row] = (one + two).astype(BF)


def piece_kernel(info_ref, ours, theirs, *outs):
    x = info_ref[1]
    for k in range(NX):
        tokens = pl.ds(pl.multiple_of(lax.rem(x + k, NX) * 16, 16), 16)
        for row in range(6):
            total = ours[row, tokens, :].astype(F4) + theirs[row, tokens, :].astype(F4)
            outs[k][row] = total.astype(BF)


def join_kernel(p0, p1, p2, p3, d0, d1, d2, d3, out):
    f = lambda r: r[...].astype(F4)
    out[:, :256] = (f(p0) + f(p1) + f(p2) + f(p3)).astype(BF)
    for r in range(6):
        for g in range(7):
            cols = slice(g * 128, (g + 1) * 128)
            total = (
                d0[r, :, cols].astype(F4)
                + d1[r, :, cols].astype(F4)
                + d2[r, :, cols].astype(F4)
                + d3[r, :, cols].astype(F4)
            )
            start = r * 112 + g * 16
            out[start : start + 16, 256:] = total.astype(BF)
    out[672:, 256:] = jnp.zeros((224, 128), BF)


def total_kernel(got_ref, out):
    total = got_ref[0:112].astype(F4)
    for k in range(1, NZ):
        total = total + got_ref[k * 112 : (k + 1) * 112].astype(F4)
    out[...] = total.astype(BF)


def final_kernel(info_ref, *refs):
    ours, theirs = refs[:7], refs[7:14]
    wkey, wvalue, dstates = refs[14:17]
    full, pool, sems = refs[17:]
    z, x, core = info_ref[0], info_ref[1], info_ref[2]
    copies = []
    for p, pieces in enumerate((ours, theirs)):
        owner = core if p == 0 else 1 - core
        for k in range(4):
            cols = pl.ds(pl.multiple_of(lax.rem(x + k, 4) * 256, 256), 256)
            tokens = pl.ds(pl.multiple_of(owner * 64 + lax.rem(x + k, 4) * 16, 16), 16)
            for m in range(8):
                if k == 0:
                    piece, base = pieces[0], m * 112
                else:
                    piece, base = pieces[2 * k - 1 + m // 4], (m % 4) * 112
                where = lax.rem(z + m, NZ)
                rows = pl.ds(pl.multiple_of(where * 112, 16), 112)
                full[p, rows, cols] = piece[base : base + 112, :256]
                for g in range(7):
                    part = slice(g * 128, (g + 1) * 128)
                    pool[where, tokens, part] = piece[base + g * 16 : base + (g + 1) * 16, 256:]
        first = pltpu.make_async_copy(full.at[p], wkey, sems.at[p])
        second = pltpu.make_async_copy(full.at[p], wvalue, sems.at[p])

        @pl.when(owner == 0)
        def _():
            first.start()

        @pl.when(owner == 1)
        def _():
            second.start()

        copies.append((owner, first, second))
    last = pltpu.make_async_copy(pool.at[:6], dstates, sems.at[2])
    last.start()
    last.wait()
    for owner, first, second in copies:

        @pl.when(owner == 0)
        def _():
            first.wait()

        @pl.when(owner == 1)
        def _():
            second.wait()


def local(queries, d_out, states, w_key, w_value, nbr_owner, nbr_row):
    me = lax.axis_index("enc").astype(jnp.int32)
    ctx = lax.axis_index("ctx").astype(jnp.int32)
    z, x, core = ctx // 8, (ctx // 2) % NX, ctx % 2
    token_count, head_width = queries.shape
    margin = SPAN - 1
    z_groups = [[zz * 8 + rest for zz in range(NZ)] for rest in range(8)]
    swap_z = lambda a: lax.all_to_all(
        a, "ctx", split_axis=0, concat_axis=0, tiled=True, axis_index_groups=z_groups
    )

    own = pl.pallas_call(
        pick_kernel,
        out_shape=near((2, 128, 896)),
        in_specs=[ANYS] * 3,
        out_specs=VMEM,
        scratch_shapes=[pltpu.SMEM((2, 2), jnp.int32), pltpu.SMEM((2, 2), jnp.int32)]
        + [pltpu.SemaphoreType.DMA((4,))],
        compiler_params=limit(8),
    )(far(nbr_owner), far(nbr_row), far(states))
    low = to_y(own, 1)
    high = to_y(own, -1)
    across = to_y(own, 2)

    owners = nbr_owner.reshape(-1)
    rows_in = nbr_row.reshape(-1)
    order = jnp.arange(4, dtype=jnp.int32)
    rank = jnp.sum(
        ((owners[:, None] == owners[None, :]) & (order[None, :] < order[:, None])).astype(jnp.int32),
        axis=1,
    )
    slots = jnp.remainder(owners - me, NY) * 2 + rank
    mine = (owners[None, :] == me) & (rank[None, :] == order[:2, None])
    owned = jnp.sum(jnp.where(mine, rows_in[None, :] + 1, 0), axis=1) - 1
    rel = [jnp.remainder(x + k, NX) for k in ORDER]
    info = jnp.concatenate([jnp.stack(rel + [core]), slots]).astype(jnp.int32)
    places = jnp.concatenate([jnp.stack([z, x, core]), owned]).astype(jnp.int32)

    late_q, late_g = after(queries, low), after(d_out, low)
    tail_q, tail_g = (
        lax.ppermute(a[:margin], "ctx", [(i, i - 1) for i in range(1, NZ * NX * 2)])
        for a in (late_q, late_g)
    )
    q_rows = jnp.concatenate([late_q[margin:], tail_q], 0)
    g_rows = jnp.concatenate([late_g[margin:], tail_g], 0)
    fetched = pl.pallas_call(
        fetch_kernel,
        out_shape=[near((896, 1024)), near((896, 1024))],
        in_specs=[ANYS] * 2,
        out_specs=[VMEM] * 2,
        scratch_shapes=[pltpu.SemaphoreType.DMA((2,))],
        compiler_params=limit(8),
    )(far(after(w_key, low)), far(after(w_value, low)))

    rows, turned = call(
        rows_kernel,
        [near((512, 896)), near((896, 512))],
        [info],
        [own, high, across, low],
    )
    turned_other = to_core(turned)
    keep, send, dq, s0, s1, s2, s3 = call(
        main_kernel,
        [near((4, 512, 256)), near((4, 512, 256)), shape((128, 1024))] + [shape((2, 128, 896))] * 4,
        [info],
        [rows, *fetched, q_rows, g_rows],
        [pltpu.VMEM((512, 1024), BF), pltpu.VMEM((512, 1024), BF), pltpu.VMEM((512, 896), F4)],
        20,
    )
    got = to_core(send)
    e1 = to_y(s1, 1)
    e3 = to_y(s3, -1)
    e2 = to_y(s2, 2)

    def weights(which, keep):
        return call(
            functools.partial(weight_kernel, which),
            [near((896, 256))] * len(which),
            [],
            [turned, turned_other, keep, got],
        )

    p2, p1, p3 = weights((0, 1, 2), keep)
    (p0,) = weights((3,), after(keep, p2))
    p2, p1, p3 = to_x(p2, 2), to_x(p1, 1), to_x(p3, -1)

    e1, e2, e3, p0, p1, p2 = lax.optimization_barrier((e1, e2, e3, p0, p1, p2))
    ours, theirs = pl.pallas_call(
        slot_kernel,
        out_shape=[near((6, 64, 896))] * 2,
        in_specs=[SMEM] + [VMEM] * 4,
        out_specs=[VMEM] * 2,
        compiler_params=limit(8),
    )(places, s0, e1, e2, e3)
    theirs = to_core(theirs)
    d0, d1, d2, d3 = call(piece_kernel, [near((6, 16, 896))] * 4, [places], [ours, theirs])
    d1 = to_x(d1, 1)
    d3 = to_x(d3, -1)
    d2 = to_x(d2, 2)
    dq = after(dq, theirs)
    earlier = lax.ppermute(
        dq[token_count - margin :], "ctx", [(i, i + 1) for i in range(NZ * NX * 2 - 1)]
    )
    d1, d2, d3, earlier = lax.optimization_barrier((d1, d2, d3, earlier))
    (joined,) = call(join_kernel, [near((896, 384))], [], [p0, p1, p2, p3, d0, d1, d2, d3])
    d_query = jnp.concatenate([earlier, dq[: token_count - margin]], 0)
    (total,) = call(total_kernel, [near((112, 384))], [], [swap_z(joined)])

    up = [to_z(total, -1)]
    down = [to_z(total, 1)]
    up[0], d_query = lax.optimization_barrier((up[0], d_query))
    for _ in range(2):
        up.append(to_z(up[-1], -1))
        down.append(to_z(down[-1], 1))
    middle = [to_z(up[-1][:64], -1), to_z(down[-1][64:], 1)]
    own = jnp.concatenate([total] + up + middle + down[::-1], 0)
    half = 448
    low_t = to_x(own[:half], 1)
    high_b = to_x(own[half:], -1)
    low_b = to_x(own[half:], 1)
    high_t = to_x(own[:half], -1)
    far_t = to_x(low_t, 1)
    far_b = to_x(high_b, -1)
    ours = [own, high_t, high_b, far_t, far_b, low_t, low_b]
    own, high_t, high_b, low_t, low_b = lax.optimization_barrier(
        (own, high_t, high_b, low_t, low_b)
    )
    theirs = [to_core(a) for a in (own, high_t, high_b, far_t, far_b, low_t, low_b)]
    arrays = ours + theirs
    d_wkey, d_wvalue, d_states = pl.pallas_call(
        final_kernel,
        out_shape=[shape((896, 1024)), shape((896, 1024)), shape((6, 128, 896))],
        in_specs=[SMEM] + [VMEM] * 14,
        out_specs=[ANYS] * 3,
        scratch_shapes=[pltpu.VMEM((2, 896, 1024), BF), pltpu.VMEM((8, 128, 896), BF)]
        + [pltpu.SemaphoreType.DMA((3,))],
        compiler_params=limit(8),
    )(places, *[pltpu.with_memory_space_constraint(a, pltpu.VMEM) for a in arrays])
    return d_query, d_states, d_wkey, d_wvalue


def solution(mesh):
    return jax.shard_map(
        local,
        mesh=mesh,
        in_specs=(
            P("ctx", "enc"),
            P("ctx", "enc"),
            P("enc", None, None),
            P(None, "enc"),
            P(None, "enc"),
            P("ctx", None),
            P("ctx", None),
        ),
        out_specs=(P("ctx", "enc"), P("enc", None, None), P(None, "enc"), P(None, "enc")),
        check_vma=False,
    )
```

```python
import functools
import math

import jax
import jax.numpy as jnp
from jax import lax
from jax.experimental import pallas as pl
from jax.experimental.pallas import tpu as pltpu
from jax.sharding import PartitionSpec as P

HEAD = 128
SPAN = 64
NX, NZ, NY = 4, 8, 4
BF = jnp.bfloat16
F4 = jnp.float32
VMEM = pl.BlockSpec(memory_space=pltpu.VMEM)
SMEM = pl.BlockSpec(memory_space=pltpu.SMEM)
ANYS = pl.BlockSpec(memory_space=pl.ANY)
ORDER = (2, 1, 3, 0)


def move(a, place):
    pairs = []
    for i in range(NZ * NX * 2):
        z, x, c = place(i // 8, (i // 2) % NX, i % 2)
        pairs.append((i, (z % NZ) * 8 + (x % NX) * 2 + c))
    return lax.ppermute(a, "ctx", pairs)


def to_x(a, k):
    return move(a, lambda z, x, c: (z, x + k, c))


def to_z(a, k):
    return move(a, lambda z, x, c: (z + k, x, c))


def to_core(a):
    return move(a, lambda z, x, c: (z, x, 1 - c))


def to_y(a, k):
    return lax.ppermute(a, "enc", [(i, (i + k) % NY) for i in range(NY)])


def shape(dims, dtype=BF):
    return jax.ShapeDtypeStruct(dims, dtype)


def after(a, *others):
    return lax.optimization_barrier((a, *others))[0]


def limit(mib):
    return pltpu.CompilerParams(vmem_limit_bytes=mib * 1024 * 1024)


def far(a):
    return pltpu.with_memory_space_constraint(a, pltpu.HBM)


def near(dims, dtype=BF):
    return pltpu.VMEM(dims, dtype)


def call(kernel, outs, scalars, arrays, scratch=(), mib=8):
    arrays = [pltpu.with_memory_space_constraint(a, pltpu.VMEM) for a in arrays]
    return pl.pallas_call(
        kernel,
        out_shape=outs,
        in_specs=[SMEM] * len(scalars) + [VMEM] * len(arrays),
        out_specs=[VMEM] * len(outs),
        scratch_shapes=list(scratch),
        compiler_params=limit(mib),
    )(*scalars, *arrays)


def dot(a, b, da, db):
    return lax.dot_general(a, b, (((da,), (db,)), ((), ())), preferred_element_type=F4)


def pick_kernel(owner_ref, row_ref, states_ref, out0, out1, owners, rows, sems):
    a = pltpu.make_async_copy(owner_ref, owners, sems.at[0])
    b = pltpu.make_async_copy(row_ref, rows, sems.at[1])
    a.start()
    b.start()
    a.wait()
    b.wait()
    me = lax.axis_index("enc")
    seen = jnp.int32(0)
    first = jnp.int32(0)
    second = jnp.int32(0)
    for u in range(4):
        hit = owners[u // 2, u % 2] == me
        row = rows[u // 2, u % 2]
        first = jnp.where(hit & (seen == 0), row, first)
        second = jnp.where(hit & (seen == 1), row, second)
        seen = seen + hit.astype(jnp.int32)
    a = pltpu.make_async_copy(states_ref.at[first], out0, sems.at[2])
    b = pltpu.make_async_copy(states_ref.at[second], out1, sems.at[3])
    a.start()
    b.start()
    a.wait()
    b.wait()


def fetch_kernel(*refs):
    sources, outs, sems = refs[:2], refs[2:4], refs[4]
    copies = [pltpu.make_async_copy(a, b, sems.at[n]) for n, (a, b) in enumerate(zip(sources, outs))]
    for copy in copies:
        copy.start()
    for copy in copies:
        copy.wait()


def rows_kernel(info_ref, *refs):
    slots, rows_ref, turned_ref = refs[:8], refs[8], refs[9]
    for u in range(4):
        for s in range(8):

            @pl.when(info_ref[5 + u] == s)
            def _():
                rows_ref[u * 128 : (u + 1) * 128, :] = slots[s][...]

    turned_ref[...] = rows_ref[...].T


def main_kernel(info_ref, *refs):
    rows_in, wk_ref, wv_ref, q_ref, g_ref = refs[:5]
    keep_ref, send_ref, dq_ref = refs[5:8]
    slot_outs = refs[8:12]
    dk_ref, dv_ref, acc_ref = refs[12:]
    scaling = 1.0 / math.sqrt(HEAD)
    core = info_ref[4]
    rows = rows_in[...]
    @pl.loop(0, 2)
    def _(pair):
        combos = []
        for m in range(2):
            j = 2 * pair + m
            cols = pl.ds(pl.multiple_of(info_ref[j] * 256, 256), 256)
            keys = dot(rows, wk_ref[:, cols], 1, 0).astype(BF)
            values = dot(rows, wv_ref[:, cols], 1, 0).astype(BF)
            q_all = q_ref[:, cols]
            g_all = g_ref[:, cols]
            for s in range(2):
                for h in range(2):
                    here = slice(h * HEAD, (h + 1) * HEAD)
                    span = slice(s * SPAN, (s + 1) * SPAN)
                    uses = slice(s * 256, (s + 1) * 256)
                    combos.append(
                        (q_all[span, here], g_all[span, here], keys[uses, here], values[uses, here])
                    )
        scores = [dot(q, k, 1, 1) for q, g, k, v in combos]
        soft_grads = [dot(g, v, 1, 1) for q, g, k, v in combos]
        terms = [jnp.exp(a * scaling) for a in scores]
        softs = [e / jnp.sum(e, axis=-1, keepdims=True) for e in terms]
        rounded = [a.astype(BF) for a in softs]
        deltas = [
            jnp.sum(r.astype(F4) * d, axis=-1, keepdims=True) for r, d in zip(rounded, soft_grads)
        ]
        grads = [(p * (d - t)).astype(BF) for p, d, t in zip(softs, soft_grads, deltas)]
        dvs = [dot(r, c[1], 0, 0).astype(BF) for r, c in zip(rounded, combos)]
        dqs = [(dot(d, c[2], 1, 0) * scaling).astype(BF) for d, c in zip(grads, combos)]
        dks = [(dot(d, c[0], 0, 0) * scaling).astype(BF) for d, c in zip(grads, combos)]
        for m in range(2):
            j = 2 * pair + m
            cols = pl.ds(pl.multiple_of(info_ref[j] * 256, 256), 256)

            def join(parts):
                one, two = parts[4 * m : 4 * m + 2], parts[4 * m + 2 : 4 * m + 4]
                return jnp.concatenate(
                    [jnp.concatenate(one, axis=1), jnp.concatenate(two, axis=1)], axis=0
                )

            dq_ref[:, cols] = join(dqs)
            dk = join(dks)
            dv = join(dvs)
            dk_ref[:, cols] = dk
            dv_ref[:, cols] = dv
            keep_ref[j] = jnp.where(core == 0, dk, dv)
            send_ref[j] = jnp.where(core == 0, dv, dk)

    acc_ref[...] = dot(dk_ref[...], wk_ref[...], 1, 1) + dot(dv_ref[...], wv_ref[...], 1, 1)
    for o, out in enumerate(slot_outs):
        for r in range(2):
            out[r] = jnp.zeros((128, 896), BF)
            for u in range(4):

                @pl.when(info_ref[5 + u] == o * 2 + r)
                def _():
                    out[r] = acc_ref[u * 128 : (u + 1) * 128, :].astype(BF)


def weight_kernel(which, turned_ref, other_ref, keep_ref, got_ref, *outs):
    turned = turned_ref[...]
    other = other_ref[...]
    for n, k in enumerate(which):
        total = dot(turned, keep_ref[k], 1, 0) + dot(other, got_ref[k], 1, 0)
        outs[n][...] = total.astype(BF)


def slot_kernel(info_ref, s0, s1, s2, s3, ours, theirs):
    core = info_ref[2]
    for out, side in ((ours, core), (theirs, 1 - core)):
        tokens = pl.ds(pl.multiple_of(side * 64, 64), 64)
        f = lambda r, n: r[n, tokens, :].astype(F4)
        sums = [f(s0, n) + f(s1, n) + f(s2, n) + f(s3, n) for n in range(2)]
        for row in range(6):
            one = jnp.where(info_ref[3] == row, sums[0], 0.0)
            two = jnp.where(info_ref[4] == row, sums[1], 0.0)
            out[row] = (one + two).astype(BF)


def piece_kernel(info_ref, ours, theirs, *outs):
    x = info_ref[1]
    for k in range(NX):
        tokens = pl.ds(pl.multiple_of(lax.rem(x + k, NX) * 16, 16), 16)
        for row in range(6):
            total = ours[row, tokens, :].astype(F4) + theirs[row, tokens, :].astype(F4)
            outs[k][row] = total.astype(BF)


def join_kernel(p0, p1, p2, p3, d0, d1, d2, d3, out):
    f = lambda r: r[...].astype(F4)
    out[:, :256] = (f(p0) + f(p1) + f(p2) + f(p3)).astype(BF)
    for r in range(6):
        for g in range(7):
            cols = slice(g * 128, (g + 1) * 128)
            total = (
                d0[r, :, cols].astype(F4)
                + d1[r, :, cols].astype(F4)
                + d2[r, :, cols].astype(F4)
                + d3[r, :, cols].astype(F4)
            )
            start = r * 112 + g * 16
            out[start : start + 16, 256:] = total.astype(BF)
    out[672:, 256:] = jnp.zeros((224, 128), BF)


def total_kernel(got_ref, out):
    total = got_ref[0:112].astype(F4)
    for k in range(1, NZ):
        total = total + got_ref[k * 112 : (k + 1) * 112].astype(F4)
    out[...] = total.astype(BF)


def final_kernel(info_ref, *refs):
    ours, theirs = refs[:7], refs[7:14]
    wkey, wvalue, dstates = refs[14:17]
    full, pool, sems = refs[17:]
    z, x, core = info_ref[0], info_ref[1], info_ref[2]
    copies = []
    for p, pieces in enumerate((ours, theirs)):
        owner = core if p == 0 else 1 - core
        for k in range(4):
            cols = pl.ds(pl.multiple_of(lax.rem(x + k, 4) * 256, 256), 256)
            tokens = pl.ds(pl.multiple_of(owner * 64 + lax.rem(x + k, 4) * 16, 16), 16)
            for m in range(8):
                if k == 0:
                    piece, base = pieces[0], m * 112
                else:
                    piece, base = pieces[2 * k - 1 + m // 4], (m % 4) * 112
                where = lax.rem(z + m, NZ)
                rows = pl.ds(pl.multiple_of(where * 112, 16), 112)
                full[p, rows, cols] = piece[base : base + 112, :256]
                for g in range(7):
                    part = slice(g * 128, (g + 1) * 128)
                    pool[where, tokens, part] = piece[base + g * 16 : base + (g + 1) * 16, 256:]
        first = pltpu.make_async_copy(full.at[p], wkey, sems.at[p])
        second = pltpu.make_async_copy(full.at[p], wvalue, sems.at[p])

        @pl.when(owner == 0)
        def _():
            first.start()

        @pl.when(owner == 1)
        def _():
            second.start()

        copies.append((owner, first, second))
    last = pltpu.make_async_copy(pool.at[:6], dstates, sems.at[2])
    last.start()
    last.wait()
    for owner, first, second in copies:

        @pl.when(owner == 0)
        def _():
            first.wait()

        @pl.when(owner == 1)
        def _():
            second.wait()


def local(queries, d_out, states, w_key, w_value, nbr_owner, nbr_row):
    me = lax.axis_index("enc").astype(jnp.int32)
    ctx = lax.axis_index("ctx").astype(jnp.int32)
    z, x, core = ctx // 8, (ctx // 2) % NX, ctx % 2
    token_count, head_width = queries.shape
    margin = SPAN - 1
    z_groups = [[zz * 8 + rest for zz in range(NZ)] for rest in range(8)]
    swap_z = lambda a: lax.all_to_all(
        a, "ctx", split_axis=0, concat_axis=0, tiled=True, axis_index_groups=z_groups
    )

    own0, own1 = pl.pallas_call(
        pick_kernel,
        out_shape=(near((128, 896)), near((128, 896))),
        in_specs=[ANYS] * 3,
        out_specs=(VMEM, VMEM),
        scratch_shapes=[pltpu.SMEM((2, 2), jnp.int32), pltpu.SMEM((2, 2), jnp.int32)]
        + [pltpu.SemaphoreType.DMA((4,))],
        compiler_params=limit(8),
    )(far(nbr_owner), far(nbr_row), far(states))
    low0 = to_y(own0, 1)
    high1 = to_y(own1, -1)
    low1 = to_y(own1, 1)
    high0 = to_y(own0, -1)
    far0 = to_y(low0, 1)
    far1 = to_y(high1, -1)

    owners = nbr_owner.reshape(-1)
    rows_in = nbr_row.reshape(-1)
    order = jnp.arange(4, dtype=jnp.int32)
    rank = jnp.sum(
        ((owners[:, None] == owners[None, :]) & (order[None, :] < order[:, None])).astype(jnp.int32),
        axis=1,
    )
    slots = jnp.remainder(owners - me, NY) * 2 + rank
    mine = (owners[None, :] == me) & (rank[None, :] == order[:2, None])
    owned = jnp.sum(jnp.where(mine, rows_in[None, :] + 1, 0), axis=1) - 1
    rel = [jnp.remainder(x + k, NX) for k in ORDER]
    info = jnp.concatenate([jnp.stack(rel + [core]), slots]).astype(jnp.int32)
    places = jnp.concatenate([jnp.stack([z, x, core]), owned]).astype(jnp.int32)

    late_q, late_g = after(queries, low1), after(d_out, low1)
    tail_q, tail_g = (
        lax.ppermute(a[:margin], "ctx", [(i, i - 1) for i in range(1, NZ * NX * 2)])
        for a in (late_q, late_g)
    )
    q_rows = jnp.concatenate([late_q[margin:], tail_q], 0)
    g_rows = jnp.concatenate([late_g[margin:], tail_g], 0)
    fetched = pl.pallas_call(
        fetch_kernel,
        out_shape=[near((896, 1024)), near((896, 1024))],
        in_specs=[ANYS] * 2,
        out_specs=[VMEM] * 2,
        scratch_shapes=[pltpu.SemaphoreType.DMA((2,))],
        compiler_params=limit(8),
    )(far(after(w_key, low0)), far(after(w_value, low0)))

    rows, turned = call(
        rows_kernel,
        [near((512, 896)), near((896, 512))],
        [info],
        [own0, own1, high0, high1, far0, far1, low0, low1],
    )
    turned_other = to_core(turned)
    keep, send, dq, s0, s1, s2, s3 = call(
        main_kernel,
        [near((4, 512, 256)), near((4, 512, 256)), shape((128, 1024))] + [shape((2, 128, 896))] * 4,
        [info],
        [rows, *fetched, q_rows, g_rows],
        [pltpu.VMEM((512, 1024), BF), pltpu.VMEM((512, 1024), BF), pltpu.VMEM((512, 896), F4)],
        20,
    )
    got = to_core(send)
    e1 = to_y(s1, 1)
    e3 = to_y(s3, -1)
    e2 = to_y(s2, 2)

    def weights(which, keep):
        return call(
            functools.partial(weight_kernel, which),
            [near((896, 256))] * len(which),
            [],
            [turned, turned_other, keep, got],
        )

    p2, p1, p3 = weights((0, 1, 2), keep)
    (p0,) = weights((3,), after(keep, p2))
    p2, p1, p3 = to_x(p2, 2), to_x(p1, 1), to_x(p3, -1)

    e1, e2, e3, p0, p1, p2 = lax.optimization_barrier((e1, e2, e3, p0, p1, p2))
    ours, theirs = pl.pallas_call(
        slot_kernel,
        out_shape=[near((6, 64, 896))] * 2,
        in_specs=[SMEM] + [VMEM] * 4,
        out_specs=[VMEM] * 2,
        compiler_params=limit(8),
    )(places, s0, e1, e2, e3)
    theirs = to_core(theirs)
    d0, d1, d2, d3 = call(piece_kernel, [near((6, 16, 896))] * 4, [places], [ours, theirs])
    d1 = to_x(d1, 1)
    d3 = to_x(d3, -1)
    d2 = to_x(d2, 2)
    dq = after(dq, theirs)
    earlier = lax.ppermute(
        dq[token_count - margin :], "ctx", [(i, i + 1) for i in range(NZ * NX * 2 - 1)]
    )
    d1, d2, d3, earlier = lax.optimization_barrier((d1, d2, d3, earlier))
    (joined,) = call(join_kernel, [near((896, 384))], [], [p0, p1, p2, p3, d0, d1, d2, d3])
    d_query = jnp.concatenate([earlier, dq[: token_count - margin]], 0)
    (total,) = call(total_kernel, [near((112, 384))], [], [swap_z(joined)])

    up = [to_z(total, -1)]
    down = [to_z(total, 1)]
    up[0], d_query = lax.optimization_barrier((up[0], d_query))
    for _ in range(2):
        up.append(to_z(up[-1], -1))
        down.append(to_z(down[-1], 1))
    middle = [to_z(up[-1][:64], -1), to_z(down[-1][64:], 1)]
    own = jnp.concatenate([total] + up + middle + down[::-1], 0)
    half = 448
    low_t = to_x(own[:half], 1)
    high_b = to_x(own[half:], -1)
    low_b = to_x(own[half:], 1)
    high_t = to_x(own[:half], -1)
    far_t = to_x(low_t, 1)
    far_b = to_x(high_b, -1)
    ours = [own, high_t, high_b, far_t, far_b, low_t, low_b]
    own, high_t, high_b, low_t, low_b = lax.optimization_barrier(
        (own, high_t, high_b, low_t, low_b)
    )
    theirs = [to_core(a) for a in (own, high_t, high_b, far_t, far_b, low_t, low_b)]
    arrays = ours + theirs
    d_wkey, d_wvalue, d_states = pl.pallas_call(
        final_kernel,
        out_shape=[shape((896, 1024)), shape((896, 1024)), shape((6, 128, 896))],
        in_specs=[SMEM] + [VMEM] * 14,
        out_specs=[ANYS] * 3,
        scratch_shapes=[pltpu.VMEM((2, 896, 1024), BF), pltpu.VMEM((8, 128, 896), BF)]
        + [pltpu.SemaphoreType.DMA((3,))],
        compiler_params=limit(8),
    )(places, *[pltpu.with_memory_space_constraint(a, pltpu.VMEM) for a in arrays])
    return d_query, d_states, d_wkey, d_wvalue


def solution(mesh):
    return jax.shard_map(
        local,
        mesh=mesh,
        in_specs=(
            P("ctx", "enc"),
            P("ctx", "enc"),
            P("enc", None, None),
            P(None, "enc"),
            P(None, "enc"),
            P("ctx", None),
            P("ctx", None),
        ),
        out_specs=(P("ctx", "enc"), P("enc", None, None), P(None, "enc"), P(None, "enc")),
        check_vma=False,
    )
```
